1024 devices in a mesh: layer: 4 (over x), row: 16 (over y, core), col: 16 (over z).
Axes of the slice: x: 4, y: 8, z: 16, core: 2. Of those that a mesh axis runs over, the one named last changes fastest.
Arguments:
- partials: float32 [4, 1, 16, 256, 1, 16, 256], P('layer', None, 'row', None, None, 'col'), as said below
- pattern: int32 [1, 16, 2, 1, 16, 2], P(None, 'row', None, None, 'col'), may hold values from 0 to 1, as said below
Outputs:
- schur: float32 [1, 16, 4, 64, 1, 16, 256], P(None, 'row', 'layer', None, None, 'col')
- factor_panels: float32 [2, 1, 16, 256, 256], P(None, None, 'row')
The draws below stay inside these ranges and needn't reach their ends.
Inputs may be any that keep to these rules, and one draw needn't show every extreme that they name: `partials`: each layer's partial is symmetric; in their sum the leading principal submatrix of order 2 * 256 is positive definite. `pattern`: symmetric in the global tile index.
All inputs are finite; a program needn't handle non-finite values.
Results may differ from the reference program's by a relative error of at most 0.0001.
Values sent between devices are 32-bit elements; how exact they have to be, the bound alone decides.
A program may use at most 32 MiB of HBM per device.

```python
import jax
import jax.numpy as jnp
from jax import lax

W = 256
TILE = 128
NBLK = 16
LAYERS = 4
TPB = 2
N_ROW = 16
N_COL = 16


def draw_partials(key, part):
    key = jax.random.fold_in(key, 3)
    subkeys = jax.random.split(key, 2)
    front_order = NBLK * W
    noise = jnp.clip(jax.random.normal(subkeys[0], (LAYERS, front_order, front_order), jnp.float32), -4.0, 4.0)
    symmetric = (noise + jnp.transpose(noise, (0, 2, 1))) * 0.5 ** 0.5 / LAYERS ** 0.5
    diagonal = jax.random.uniform(subkeys[1], (LAYERS, front_order), jnp.float32, 4.0, 8.0) * W ** 0.5 / LAYERS
    identity = jnp.eye(front_order, dtype=jnp.float32)
    matrix = symmetric * (1.0 - identity) + identity * diagonal[:, :, None]
    return matrix.reshape(LAYERS, NBLK // N_ROW, N_ROW, W, NBLK // N_COL, N_COL, W)


def draw_pattern(key, part):
    key = jax.random.fold_in(key, 7)
    first_key, second_key = jax.random.split(key)
    tile_count = NBLK * TPB
    levels = jax.random.randint(first_key, (tile_count,), 0, 8)
    raw_draw = jax.random.randint(second_key, (tile_count, tile_count), 0, 16)
    tile_ids = jnp.arange(tile_count)
    upper_half = tile_ids[:, None] <= tile_ids[None, :]
    symmetric = jnp.where(upper_half, raw_draw, raw_draw.T)
    threshold = levels[:, None] + levels[None, :]
    tile_pattern = (symmetric < threshold).astype(jnp.int32)
    return tile_pattern.reshape(NBLK // N_ROW, N_ROW, TPB, NBLK // N_COL, N_COL, TPB)


def setup_inputs(seed: int = 0) -> dict:
    streams_of = jax.random.split(jax.random.key(seed), 3)
    return {
        "partials": draw_partials(jax.random.fold_in(streams_of[2], 71), 0),
        "pattern": draw_pattern(jax.random.fold_in(streams_of[2], 71), 0),
    }


def reference(partials, pattern):
    front_order = NBLK * W
    tile_count = NBLK * TPB
    matrix = jnp.sum(partials.astype(jnp.float32), axis=0).reshape(front_order, front_order)
    tile_pattern = pattern.reshape(tile_count, tile_count)
    tile_block = jnp.arange(tile_count) // TPB
    kept_tiles = (tile_pattern > 0) | (tile_block[:, None] < 2) | (tile_block[None, :] < 2)
    entry_keep = jnp.repeat(jnp.repeat(kept_tiles, TILE, axis=0), TILE, axis=1)
    block_ids = jnp.arange(front_order) // W
    panel_list = []
    for panel in range(2):
        start = panel * W
        diagonal = matrix[start:start + W, start:start + W]
        diag_factor = jnp.linalg.cholesky(diagonal)
        column_raw = matrix[:, start:start + W]
        lower_panel = jax.scipy.linalg.solve_triangular(diag_factor, column_raw.T, lower=True).T
        lower_panel = jnp.where(block_ids[:, None] > panel, lower_panel, 0.0)
        lower_panel = lower_panel.at[start:start + W].set(diag_factor)
        row_raw = matrix[start:start + W, :]
        upper_panel = jax.scipy.linalg.solve_triangular(diag_factor, row_raw, lower=True)
        upper_panel = jnp.where(block_ids[None, :] > panel, upper_panel, 0.0)
        product = jnp.dot(lower_panel.astype(jnp.float32), upper_panel.astype(jnp.float32), precision=lax.Precision.HIGHEST, preferred_element_type=jnp.float32)
        matrix = matrix - jnp.where(entry_keep, product, 0.0)
        panel_list.append(lower_panel)
    schur = matrix.reshape(NBLK // N_ROW, N_ROW, LAYERS, W // LAYERS, NBLK // N_COL, N_COL, W)
    factor_panels = jnp.stack(panel_list).reshape(2, NBLK // N_ROW, N_ROW, W, W)
    return (schur, factor_panels)
```

```python
import jax
import jax.numpy as jnp
from jax import lax
from jax.experimental import pallas as pl
from jax.experimental.pallas import tpu as pltpu
from jax.sharding import PartitionSpec as P

MESH = pl.DeviceIdType.MESH
EXACT = lax.Precision.HIGHEST
F32 = jnp.float32


def dot(a, b):
    return lax.dot_general(a, b, (((1,), (0,)), ((), ())), precision=EXACT, preferred_element_type=F32)


def dot_t(a, b):
    return lax.dot_general(a, b, (((1,), (1,)), ((), ())), precision=EXACT, preferred_element_type=F32)


def exchange(
    part, slab, prow, qcol, lead,
    xin, x_send, x_recv, z_send, z_recv, y_send, yd_send, y_recv, yd_recv,
    g_send, g_recv, w_send, w_recv,
):
    l = lax.axis_index("layer")
    r = lax.axis_index("row")
    c = lax.axis_index("col")
    core = lax.rem(r, 2)
    other = r + 1 - 2 * core
    peers = [lax.rem(l + d, 4) for d in (1, 2, 3)]
    sources = [lax.rem(l + 4 - d, 4) for d in (1, 2, 3)]

    barrier = pltpu.get_barrier_semaphore()

    def greet(device):
        pl.semaphore_signal(barrier, inc=1, device_id=device, device_id_type=MESH)

    for k in range(2):
        @pl.when(c != k)
        def _():
            greet((l, r, k))

    @pl.when(r >= 2)
    def _():
        greet((l, core, c))

    for peer in peers:
        greet((peer, r, c))
    greet((l, other, c))
    waits = 4 + jnp.where(c < 2, 15, 0) + jnp.where(r < 2, 7, 0)
    pl.semaphore_wait(barrier, waits)

    def x_copy(i, peer):
        return pltpu.make_async_remote_copy(
            src_ref=part.at[pl.ds(pl.multiple_of(peer * 64, 64), 64)],
            dst_ref=xin.at[l],
            send_sem=x_send.at[i], recv_sem=x_recv.at[i],
            device_id=(peer, r, c), device_id_type=MESH,
        )

    x_copies = [x_copy(i, peer) for i, peer in enumerate(peers)]
    for copy in x_copies:
        copy.start()
    xin[l] = part[pl.ds(pl.multiple_of(l * 64, 64), 64), :]
    for copy in x_copies:
        copy.wait_recv()
    total = (xin[0] + xin[1]) + (xin[2] + xin[3])
    slab[...] = total

    def z_copy(i, k):
        return pltpu.make_async_remote_copy(
            src_ref=slab, dst_ref=prow.at[k, l],
            send_sem=z_send.at[i], recv_sem=z_recv.at[k],
            device_id=(l, r, lax.rem(c + Z_ORDER[i], 16)), device_id_type=MESH,
        )

    for k in range(2):
        @pl.when(c == k)
        def _():
            for i in range(15):
                z_copy(i, k).start()
            prow[k, l] = total

    def y_copy(i, k):
        return pltpu.make_async_remote_copy(
            src_ref=slab, dst_ref=qcol.at[k, l],
            send_sem=y_send.at[i], recv_sem=y_recv,
            device_id=(l, lax.rem(r + 2 * Y_ORDER[i], 16), c), device_id_type=MESH,
        )

    for k in range(2):
        @pl.when(r == k)
        def _():
            for i in range(7):
                y_copy(i, k).start()
            qcol[k, l] = total

    def yd_copy(i, src, dst, s):
        return pltpu.make_async_remote_copy(
            src_ref=prow.at[src, l], dst_ref=lead.at[dst, l],
            send_sem=yd_send.at[s, i], recv_sem=yd_recv.at[s],
            device_id=(l, lax.rem(r + 2 * Y_ORDER[i], 16), c), device_id_type=MESH,
        )

    for k in range(2):
        @pl.when(c != k)
        def _():
            z_copy(0, k).wait_recv()

        for owner, dst in (((0, 0), (1, 1)) if k == 0 else ((1, 2),)):
            @pl.when(r == owner)
            def _():
                for i in range(7):
                    yd_copy(i, k, dst, k).start()
                lead[dst, l] = prow[k, l]

    @pl.when(r >= 2)
    def _():
        yd_copy(0, 0, 0, 0).wait_recv()

        @pl.when(core == 1)
        def _():
            yd_copy(0, 1, 2, 1).wait_recv()

    def g_copy(i, ref, j):
        return pltpu.make_async_remote_copy(
            src_ref=ref, dst_ref=ref,
            send_sem=g_send.at[j, i], recv_sem=g_recv.at[j, i],
            device_id=(peers[i], r, c), device_id_type=MESH,
        )

    def g_all(ref, j):
        return [g_copy(i, ref, j) for i in range(3)]

    lead_of = ((0,), (1, 2))
    for k in range(2):
        @pl.when(core == k)
        def _():
            for j, b in enumerate(lead_of[k]):
                for copy in g_all(lead.at[b, l], j):
                    copy.start()
    for k in range(2):
        for copy in g_all(prow.at[k, l], 2 + k):
            copy.start()

    @pl.when(r >= 2)
    def _():
        y_copy(0, 0).wait_recv()

    for k in range(2):
        @pl.when(core == k)
        def _():
            for copy in g_all(qcol.at[k, l], 4):
                copy.start()

    def w_copy(ref, j):
        return pltpu.make_async_remote_copy(
            src_ref=ref, dst_ref=ref, send_sem=w_send.at[j], recv_sem=w_recv.at[j],
            device_id=(l, other, c), device_id_type=MESH,
        )

    for k in range(2):
        @pl.when(core == k)
        def _():
            for j, b in enumerate(lead_of[k]):
                for copy in g_all(lead.at[b, l], j):
                    copy.wait_recv()
                w_copy(lead.at[b], j).start()
            for copy in g_all(qcol.at[k, l], 4):
                copy.wait_recv()
            w_copy(qcol.at[k], 2).start()
    for k in range(2):
        for copy in g_all(prow.at[k, l], 2 + k):
            copy.wait_recv()
    for k in range(2):
        @pl.when(core == k)
        def _():
            for j, b in enumerate(lead_of[1 - k]):
                w_copy(lead.at[b], j).wait_recv()
            w_copy(qcol.at[1 - k], 2).wait_recv()
            for j, b in enumerate(lead_of[k]):
                for copy in g_all(lead.at[b, l], j):
                    copy.wait_send()
                w_copy(lead.at[b], j).wait_send()
            for copy in g_all(qcol.at[k, l], 4):
                copy.wait_send()
            w_copy(qcol.at[k], 2).wait_send()
    for k in range(2):
        for copy in g_all(prow.at[k, l], 2 + k):
            copy.wait_send()
    for copy in x_copies:
        copy.wait_send()

    @pl.when(c < 2)
    def _():
        for i in range(15):
            z_copy(i, 0).wait_send()

    @pl.when(r < 2)
    def _():
        for i in range(7):
            y_copy(i, 0).wait_send()
            yd_copy(i, 0, 0, 0).wait_send()

    @pl.when(r == 1)
    def _():
        for i in range(7):
            yd_copy(i, 1, 2, 1).wait_send()


Z_ORDER = (8, 7, 9, 6, 10, 5, 11, 4, 12, 3, 13, 2, 14, 1, 15)
Y_ORDER = (4, 3, 5, 2, 6, 1, 7)


def lanes(x, k):
    return jnp.broadcast_to(x[:, k : k + 1], (8, 128))


def rows(x, k):
    return jnp.broadcast_to(x[k : k + 1, :], (8, 128))


def factor_tile(tile):
    lane = lax.broadcasted_iota(jnp.int32, (8, 128), 1)
    sub = lax.broadcasted_iota(jnp.int32, (8, 128), 0)
    x = [tile[8 * g : 8 * g + 8, :] for g in range(16)]
    upper, inverse = [], []
    for b in range(16):
        base = 8 * b
        y = x[b]
        cols = [lanes(y, base + k) for k in range(8)]
        z = jnp.where(lane < base, y, jnp.where(lane == base + sub, 1.0, 0.0))
        entry = {}
        recip = []
        pivots = None
        for j in range(8):
            d = rows(cols[j], j)
            pivots = d if pivots is None else jnp.where(sub >= j, d, pivots)
            recip.append(1.0 / d)
            if j < 7:
                m = jnp.where(sub > j, cols[j], 0.0) * recip[j]
                for k in range(j + 1, 8):
                    entry[j, k] = rows(cols[k], j)
                    cols[k] = cols[k] - m * entry[j, k]
                y = y - m * rows(y, j)
                z = z - m * rows(z, j)
        scale = lax.rsqrt(pivots)
        upper.append(jnp.where(lane >= base + sub, y * scale, 0.0))
        inverse.append(z * scale)
        if b < 15:
            v = jnp.where(lane < base + 8, z, y)
            v_rows = [rows(v, j) for j in range(8)]
            inside = (lane >= base) & (lane < base + 8)
            for g in range(b + 1, 16):
                cg = [lanes(x[g], base + k) for k in range(8)]
                acc = jnp.where(inside, 0.0, x[g])
                for j in range(8):
                    m = cg[j] * recip[j]
                    for k in range(j + 1, 8):
                        cg[k] = cg[k] - m * entry[j, k]
                    acc = acc - m * v_rows[j]
                x[g] = acc
    return jnp.concatenate(upper, axis=0), jnp.concatenate(inverse, axis=0)


def factor_block(block):
    upper0, g0 = factor_tile(block[:128, :128])
    low = dot_t(block[128:, :128], g0)
    upper1, g1 = factor_tile(block[128:, 128:] - dot_t(low, low))
    zero = jnp.zeros((128, 128), F32)
    factor = jnp.concatenate(
        [jnp.concatenate([upper0.T, zero], axis=1), jnp.concatenate([low, upper1.T], axis=1)], axis=0
    )
    corner = -dot(g1, dot(low, g0))
    inverse = jnp.concatenate(
        [jnp.concatenate([g0, zero], axis=1), jnp.concatenate([corner, g1], axis=1)], axis=0
    )
    return factor, inverse


def eliminate(pattern, slab, prow, qcol, lead, schur, panels):
    l = lax.axis_index("layer")
    r = lax.axis_index("row")
    c = lax.axis_index("col")
    a00, a10, a11 = (lead[i].reshape(256, 256) for i in range(3))
    p0, p1 = (prow[i].reshape(256, 256) for i in range(2))
    q0, q1 = (qcol[i].reshape(256, 256) for i in range(2))
    f0, inv0 = factor_block(a00)
    l10 = dot_t(a10, inv0)
    rest = a11 - dot_t(l10, l10)
    l0 = jnp.where(r == 0, f0, dot_t(p0, inv0))
    u0 = dot(inv0, q0)
    p1 = p1 - dot_t(l0, l10)
    q1 = q1 - dot(l10, u0)
    u0 = jnp.where(c == 0, 0.0, u0)
    panels[0] = l0
    f1, inv1 = factor_block(rest)
    l1 = jnp.where(r == 0, 0.0, jnp.where(r == 1, f1, dot_t(p1, inv1)))
    u1 = jnp.where(c < 2, 0.0, dot(inv1, q1))
    panels[1] = l1
    mine = pl.ds(pl.multiple_of(l * 64, 64), 64)
    product = dot(panels[0, mine, :], u0) + dot(panels[1, mine, :], u1)
    half = lax.div(l, 2)
    lane = lax.broadcasted_iota(jnp.int32, (64, 256), 1)
    flag = jnp.where(lane < 128, pattern[half, 0], pattern[half, 1])
    keep = (flag > 0) | (r < 2) | (c < 2)
    schur[...] = slab[...] - jnp.where(keep, product, 0.0)


def on_device(partials, pattern):
    vmem = pl.BlockSpec(memory_space=pltpu.VMEM)
    dma = pltpu.SemaphoreType.DMA
    slab, prow, qcol, lead = pl.pallas_call(
        exchange,
        out_shape=[
            jax.ShapeDtypeStruct((64, 256), F32),
            jax.ShapeDtypeStruct((2, 4, 64, 256), F32),
            jax.ShapeDtypeStruct((2, 4, 64, 256), F32),
            jax.ShapeDtypeStruct((3, 4, 64, 256), F32),
        ],
        in_specs=[vmem],
        out_specs=[vmem] * 4,
        scratch_shapes=[
            pltpu.VMEM((4, 64, 256), F32),
            dma((3,)), dma((3,)), dma((15,)), dma((2,)), dma((7,)), dma((2, 7)), dma, dma((2,)),
            dma((5, 3)), dma((5, 3)), dma((3,)), dma((3,)),
        ],
        compiler_params=pltpu.CompilerParams(
            collective_id=0, has_side_effects=True, vmem_limit_bytes=32 * 1024 * 1024
        ),
        name="exchange",
    )(partials.reshape(256, 256))
    schur, panels = pl.pallas_call(
        eliminate,
        out_shape=[
            jax.ShapeDtypeStruct((64, 256), F32),
            jax.ShapeDtypeStruct((2, 256, 256), F32),
        ],
        in_specs=[pl.BlockSpec(memory_space=pltpu.SMEM)] + [vmem] * 4,
        out_specs=[vmem] * 2,
        compiler_params=pltpu.CompilerParams(vmem_limit_bytes=32 * 1024 * 1024),
        name="eliminate",
    )(pattern.reshape(2, 2), slab, prow, qcol, lead)
    return schur.reshape(1, 1, 1, 64, 1, 1, 256), panels.reshape(2, 1, 1, 256, 256)


def solution(mesh):
    return jax.shard_map(
        on_device,
        mesh=mesh,
        in_specs=(
            P("layer", None, "row", None, None, "col", None),
            P(None, "row", None, None, "col", None),
        ),
        out_specs=(
            P(None, "row", "layer", None, None, "col", None),
            P(None, None, "row", None, None),
        ),
        check_vma=False,
    )
```

```python
import jax
import jax.numpy as jnp
from jax import lax
from jax.experimental import pallas as pl
from jax.experimental.pallas import tpu as pltpu
from jax.sharding import PartitionSpec as P

MESH = pl.DeviceIdType.MESH
EXACT = lax.Precision.HIGHEST
F32 = jnp.float32


def dot(a, b):
    return lax.dot_general(a, b, (((1,), (0,)), ((), ())), precision=EXACT, preferred_element_type=F32)


def dot_t(a, b):
    return lax.dot_general(a, b, (((1,), (1,)), ((), ())), precision=EXACT, preferred_element_type=F32)


def lanes(x, k):
    return jnp.broadcast_to(x[:, k : k + 1], (8, 128))


def rows(x, k):
    return jnp.broadcast_to(x[k : k + 1, :], (8, 128))


def factor_tile(tile):
    lane=lax.broadcasted_iota(jnp.int32,(8,128),1); sub=lax.broadcasted_iota(jnp.int32,(8,128),0)
    X=[tile[8*g:8*g+8,:] for g in range(16)]; FT=[];G=[]
    for b in range(0,16,2):
        base=8*b
        Y0,Y1=X[b],X[b+1]
        c0=[lanes(Y0,base+k) for k in range(8)]
        c1=[lanes(Y1,base+k) for k in range(16)]
        Z0=jnp.where(lane<base,Y0,jnp.where(lane==base+sub,1.0,0.0))
        Z1=jnp.where(lane<base,Y1,jnp.where(lane==base+8+sub,1.0,0.0))
        U={};p=[]; dv=[None,None]; pv=[None,None]
        d=rows(c0[0],0)
        for j in range(16):
            h,q=divmod(j,8)
            dv[h]=d if q==0 else jnp.where(sub>=q,d,dv[h])
            pj=1.0/d; p.append(pj)
            pv[h]=pj if q==0 else jnp.where(sub>=q,pj,pv[h])
            if j==15: break
            if h==0:
                if j<7: e1=rows(c0[j+1],j); dn=rows(c0[j+1],j+1)
                else: e1=rows(c1[j],0); dn=rows(c1[8],0)
                d=dn-(e1*pj)*e1
                m0=jnp.where(sub>j,c0[j],0.0)*pj if j<7 else None
                m1=c1[j]*pj
                for k in range(j+1,8):
                    u=rows(c0[k],j); U[j,k]=u
                    c0[k]=c0[k]-m0*u; c1[k]=c1[k]-m1*u
                for k in range(8,16):
                    u=rows(c1[j],k-8); U[j,k]=u
                    c1[k]=c1[k]-m1*u
                y=rows(Y0,j); z=rows(Z0,j)
                if j<7: Y0=Y0-m0*y; Z0=Z0-m0*z
                Y1=Y1-m1*y; Z1=Z1-m1*z
            else:
                e1=rows(c1[j+1],q); d=rows(c1[j+1],q+1)-(e1*pj)*e1
                m1=jnp.where(sub>q,c1[j],0.0)*pj
                for k in range(j+1,16):
                    u=rows(c1[k],q); U[j,k]=u
                    c1[k]=c1[k]-m1*u
                Y1=Y1-m1*rows(Y1,q); Z1=Z1-m1*rows(Z1,q)
        for h,(Y,Z) in enumerate(((Y0,Z0),(Y1,Z1))):
            rs=lax.rsqrt(dv[h])
            FT.append(jnp.where(lane>=base+8*h+sub,Y*rs,0.0)); G.append(Z*rs)
        if b<14:
            V0=jnp.where(lane<base+16,Z0,Y0); V1=jnp.where(lane<base+16,Z1,Y1)
            inb=(lane>=base)&(lane<base+16)
            for g in (b+2,b+3):
                cg=[lanes(X[g],base+k) for k in range(16)]
                acc=jnp.where(inb,0.0,X[g])
                for j in range(16):
                    m=cg[j]*p[j]
                    for k in range(j+1,16): cg[k]=cg[k]-m*U[j,k]
                    acc=acc-m*rows(V0 if j<8 else V1,j%8)
                X[g]=acc
            if b<12:
                K0=V0*pv[0]; K1=V1*pv[1]
                for j in range(15,0,-1):
                    h,q=divmod(j,8)
                    if h==1:
                        kr=rows(K1,q)
                        if q>0: K1=K1-jnp.where(sub<q,c1[j]*pv[1],0.0)*kr
                        col=U[0,j]
                        for i in range(1,8): col=jnp.where(sub>=i,U[i,j],col)
                        K0=K0-col*pv[0]*kr
                    else:
                        K0=K0-jnp.where(sub<q,c0[j]*pv[0],0.0)*rows(K0,q)
                Kr=[rows(K0,j) for j in range(8)]+[rows(K1,j) for j in range(8)]
                for g in range(b+4,16):
                    acc=jnp.where(inb,0.0,X[g])
                    for j in range(16): acc=acc-lanes(X[g],base+j)*Kr[j]
                    X[g]=acc
    return jnp.concatenate(FT,axis=0), jnp.concatenate(G,axis=0)


TREE = (
    {0: (1, 2, 5, 8, 15, 13), 2: (3, 4), 5: (6, 7), 8: (9, 10), 15: (14,), 13: (12, 11)},
    {1: (0, 2, 3, 6, 9, 14, 12), 3: (4, 5), 6: (7, 8), 9: (10,), 14: (15, 13), 12: (11,)},
)
COL_ORDER = (tuple(range(1, 16)), (0,) + tuple(range(2, 16)))
CHIP_ORDER = (4, 3, 5, 2, 6, 1, 7)
HOME = ((0, 0), (1, 0), (1, 1))
CORE = (0, 1, 0)
OWNERS = ((1, 2, 3), (0, 1, 2, 3), (0, 1, 2, 3))
THIRDS = {1: (0, 48), 2: (48, 88), 3: (88, 128)}
TILES = ((0, 0), (128, 0), (128, 128))
PARTS = ((0, 0), (0, 1), (0, 2), (1, 0), (2, 0))
FIRST = (0, 1, 2)
SECOND, THIRD = 3, 4


def parent_col(k, c):
    up = jnp.int32(0)
    for sender, cols in TREE[k].items():
        for col in cols:
            up = jnp.where(c == col, sender, up)
    return up


def piece(ref, p, owner):
    b, t = PARTS[p]
    if b == 0:
        lo, hi = THIRDS[owner]
        top, left = TILES[t]
        return ref.at[0, top + lo : top + hi, left : left + 128]
    if b == 2 and owner < 2:
        return ref.at[2, 64 * owner : 64 * owner + 64, 0:128]
    return ref.at[b, 64 * owner : 64 * owner + 64]


def kernel(
    pattern, part, schur, panels,
    xin, din, slab, prow, qcol, lead, work,
    ready_y, ready_z, ready_w, x_send, x_recv, d_send, d_recv, z_send, zn_send, z_recv, y_send, y_recv,
    zd_send, zd_recv, yd_send, yd_recv, gd_send, gd_recv, g_send, g_recv,
    w_send, w_recv, wq_send, wq_recv,
):
    l = lax.axis_index("layer")
    r = lax.axis_index("row")
    c = lax.axis_index("col")
    core = lax.rem(r, 2)
    sibling = r + 1 - 2 * core
    peers = [lax.rem(l + d, 4) for d in (1, 2, 3)]
    far_row = r >= 2
    row_role = [(l > 0) | (c > 0), c >= 0]
    col_role = [(l > 0) | (r > 0), r > 0]

    def remote(src, dst, send, recv, device):
        return pltpu.make_async_remote_copy(
            src_ref=src, dst_ref=dst, send_sem=send, recv_sem=recv, device_id=device, device_id_type=MESH
        )

    barrier = pltpu.get_barrier_semaphore()

    def greet(device):
        pl.semaphore_signal(barrier, inc=1, device_id=device, device_id_type=MESH)

    for peer in peers:
        greet((peer, r, c))

    @pl.when(core == 1)
    def _():
        greet((l, sibling, c))

    for k in range(2):
        @pl.when((c == k) & col_role[k] & jnp.logical_not(far_row))
        def _():
            for col in COL_ORDER[k]:
                greet((l, r, col))

        for sender, cols in TREE[k].items():
            @pl.when((c == sender) & far_row)
            def _():
                for col in cols:
                    greet((l, r, col))

        @pl.when((r == k) & row_role[k])
        def _():
            for y in CHIP_ORDER:
                greet((l, 2 * y + k, c))
                if k == 1:
                    greet((l, 2 * y, c))

    served_y = [far_row & row_role[0] & (core == 0), far_row & row_role[1]]
    served_z = [col_role[k] & (c != k) for k in range(2)]
    count = 3
    for flag in served_y + served_z + [core == 0]:
        count = count + jnp.where(flag, 1, 0)
    pl.semaphore_wait(barrier, count)

    def ready(sem, device):
        pl.semaphore_signal(sem, inc=1, device_id=device, device_id_type=MESH)

    for k in range(2):
        @pl.when(served_y[k])
        def _():
            ready(ready_y, (l, k, c))

        @pl.when(served_z[k])
        def _():
            ready(ready_z.at[c], (l, r, jnp.where(far_row, parent_col(k, c), k)))

    @pl.when(core == 0)
    def _():
        ready(ready_w, (l, sibling, c))

    def d_copy(owner, t):
        return remote(piece(part, t, owner), piece(din.at[l], t, owner), d_send.at[owner - 1, t], d_recv.at[t, l],
                      (owner, r, c))

    def x_copy(i):
        rows_to = pl.ds(pl.multiple_of(peers[i] * 64, 64), 64)
        return remote(part.at[0, rows_to], xin.at[l], x_send.at[i], x_recv.at[i], (peers[i], r, c))

    first = (r == 0) & (c == 0)

    @pl.when(first)
    def _():
        for t in FIRST:
            for owner in OWNERS[0]:
                @pl.when(l != owner)
                def _():
                    d_copy(owner, t).start()

    for i in range(3):
        x_copy(i).start()

    own_rows = pl.ds(pl.multiple_of(l * 64, 64), 64)
    xin[l] = part[0, own_rows]

    def yd_rows(p):
        rows_to = [2 * y + CORE[PARTS[p][0]] for y in CHIP_ORDER]
        return rows_to + [0] if p == THIRD else rows_to

    def yd_copies(p, owner):
        ref = piece(lead, p, owner)
        return [
            remote(ref, ref, yd_send.at[p, i], yd_recv.at[p], (l, row, c)) for i, row in enumerate(yd_rows(p))
        ]

    def zd_copies(p, owner):
        ref = piece(lead, p, owner)
        return [
            remote(ref, ref, zd_send.at[p, i], zd_recv.at[p], (l, r, col))
            for i, col in enumerate(COL_ORDER[HOME[PARTS[p][0]][1]])
        ]

    def gd_copies(p, owner):
        ref = piece(lead, p, owner)
        return [remote(ref, ref, gd_send.at[p, i], gd_recv.at[p, owner], (peers[i], r, c)) for i in range(3)]

    def w_copy(p, owner):
        ref = piece(lead, p, owner)
        return remote(ref, ref, w_send.at[p, owner], w_recv.at[p, owner], (l, sibling, c))

    def row_sends(p, owner):
        for row, copy in zip(yd_rows(p), yd_copies(p, owner)):
            if row == 0:
                pl.semaphore_wait(ready_w, 1)
            copy.start()

    def col_sends(p, owner, wait):
        for col, copy in zip(COL_ORDER[HOME[PARTS[p][0]][1]], zd_copies(p, owner)):
            if wait:
                pl.semaphore_wait(ready_z.at[col], 1)
            copy.start()

    for k in range(2):
        @pl.when((r == k) & row_role[k])
        def _():
            pl.semaphore_wait(ready_y, (7, 14)[k])

    def add_first():
        for owner in OWNERS[0]:
            lo, hi = THIRDS[owner]

            @pl.when(first & (l == owner))
            def _():
                for t in FIRST:
                    top, left = TILES[t]
                    total = None
                    for q in range(4):
                        if q != owner:
                            remote(piece(part, t, owner), piece(din.at[q], t, owner), d_send.at[0, t],
                                   d_recv.at[t, q], (q, r, c)).wait_recv()
                        source = part if q == owner else din.at[q]
                        term = source[0, top + lo : top + hi, left : left + 128]
                        total = term if total is None else total + term
                    lead[0, top + lo : top + hi, left : left + 128] = total
                    row_sends(t, owner)
                    col_sends(t, owner, t == 0)

    def add_slab():
        for i in range(3):
            x_copy(i).wait_recv()
        slab[...] = (xin[0] + xin[1]) + (xin[2] + xin[3])

    @pl.when(first & (l > 0))
    def _():
        add_first()

    add_slab()

    def z_copies(k):
        return {
            sender: [
                remote(slab if sender == k else prow.at[k, l], prow.at[k, l],
                       z_send.at[i] if sender == k else zn_send.at[i], z_recv.at[k], (l, r, col))
                for i, col in enumerate(cols)
            ]
            for sender, cols in TREE[k].items()
        }

    def y_copies(k):
        return [
            remote(slab, qcol.at[k, l], y_send.at[i], y_recv, (l, 2 * y + k, c)) for i, y in enumerate(CHIP_ORDER)
        ]

    for p in (SECOND, THIRD):
        b = PARTS[p][0]

        @pl.when((r == 1) & (c == HOME[b][1]))
        def _():
            lead[b, own_rows] = slab[...]
            for owner in OWNERS[b]:
                @pl.when(l == owner)
                def _():
                    row_sends(p, owner)
                    col_sends(p, owner, True)

    for k in range(2):
        @pl.when((c > 0) & (r == k))
        def _():
            qcol[k, l] = slab[...]
            for copy in y_copies(k):
                copy.start()

        @pl.when(far_row & (c == k))
        def _():
            prow[k, l] = slab[...]

    for k in (1, 0):
        for sender, cols in TREE[k].items():
            @pl.when(far_row & (c == sender))
            def _():
                copies = z_copies(k)[sender]
                if sender != k:
                    copies[0].wait_recv()
                for col, copy in zip(cols, copies):
                    pl.semaphore_wait(ready_z.at[col], 1)
                    copy.start()

    for p in (SECOND, THIRD) + FIRST:
        b = PARTS[p][0]

        @pl.when((r == HOME[b][0]) & (c != HOME[b][1]))
        def _():
            for owner in OWNERS[b]:
                @pl.when(l == owner)
                def _():
                    zd_copies(p, owner)[0].wait_recv()
                    row_sends(p, owner)

    def g_copies(ref, j):
        return [remote(ref, ref, g_send.at[j, i], g_recv.at[j, i], (peers[i], r, c)) for i in range(3)]

    def gather_panels():
        @pl.when(far_row)
        def _():
            for k in range(2):
                leaf = c != k
                for sender in TREE[k]:
                    leaf = leaf & (c != sender)

                @pl.when(leaf)
                def _():
                    z_copies(k)[k][0].wait_recv()

                for copy in g_copies(prow.at[k, l], k):
                    copy.start()

        for k in range(2):
            @pl.when((c > 0) & (core == k))
            def _():
                @pl.when(far_row)
                def _():
                    y_copies(k)[0].wait_recv()

                for copy in g_copies(qcol.at[k, l], 2):
                    copy.start()

    def gather_lead(p):
        b = PARTS[p][0]

        @pl.when(core == CORE[b])
        def _():
            for owner in OWNERS[b]:
                @pl.when(l == owner)
                def _():
                    @pl.when(far_row if b < 2 else r >= 0)
                    def _():
                        yd_copies(p, owner)[0].wait_recv()

                    for copy in gd_copies(p, owner):
                        copy.start()

    def passes(p, owner):
        return (far_row | (l != owner)) if p == THIRD else (l >= 0)

    def lead_pass(p, owner):
        b = PARTS[p][0]

        @pl.when(core == CORE[b])
        def _():
            @pl.when(l != owner)
            def _():
                gd_copies(p, owner)[0].wait_recv()

            @pl.when(passes(p, owner))
            def _():
                w_copy(p, owner).start()

    def lead_wait(p, owner):
        @pl.when((core != CORE[PARTS[p][0]]) & passes(p, owner))
        def _():
            w_copy(p, owner).wait_recv()

    def wq_copy(k):
        return remote(qcol.at[k], qcol.at[k], wq_send, wq_recv, (l, sibling, c))

    def panels_pass():
        for k in range(2):
            @pl.when((c > 0) & (core == k))
            def _():
                for copy in g_copies(qcol.at[k, l], 2):
                    copy.wait_recv()
                wq_copy(k).start()

    def panels_wait():
        @pl.when(far_row)
        def _():
            for k in range(2):
                for copy in g_copies(prow.at[k, l], k):
                    copy.wait_recv()

        for k in range(2):
            @pl.when((c > 0) & (core != k))
            def _():
                wq_copy(k).wait_recv()

    @pl.when(jnp.logical_not(far_row))
    def _():
        prow[...] = jnp.zeros_like(prow)

    @pl.when(c == 0)
    def _():
        qcol[...] = jnp.zeros_like(qcol)

    @pl.when((core == 1) & far_row)
    def _():
        pl.semaphore_wait(ready_w, 1)

    gather_panels()
    gather_lead(SECOND)
    gather_lead(THIRD)
    for p in FIRST:
        gather_lead(p)

    zero = jnp.zeros((128, 128), F32)

    def finish(upper0, g0, second, ref):
        low = dot_t(second[:, :128], g0)
        upper1, g1 = factor_tile(second[:, 128:] - dot_t(low, low))
        ref[0, 0:128, 0:128] = upper0.T
        ref[0, 0:128, 128:256] = zero
        ref[0, 128:256, 0:128] = low
        ref[0, 128:256, 128:256] = upper1.T
        ref[1, 0:128, 0:128] = g0
        ref[1, 0:128, 128:256] = zero
        ref[1, 128:256, 0:128] = -dot(g1, dot(low, g0))
        ref[1, 128:256, 128:256] = g1

    for owner in OWNERS[0]:
        lead_pass(0, owner)
    for owner in OWNERS[0]:
        lead_wait(0, owner)
    upper0, g0 = factor_tile(lead[0, 0:128, 0:128])
    for p in (1, 2):
        for owner in OWNERS[0]:
            lead_pass(p, owner)
    for p in (SECOND, THIRD):
        for owner in OWNERS[1]:
            lead_pass(p, owner)
    for p in (1, 2):
        for owner in OWNERS[0]:
            lead_wait(p, owner)
    finish(upper0, g0, lead[0, 128:256, :], work)
    panels_pass()
    for p in (SECOND, THIRD):
        for owner in OWNERS[1]:
            lead_wait(p, owner)
    inv0 = work[1]
    l10 = dot_t(lead[1], inv0)
    rest = lead[2] - dot_t(l10, l10)
    work[2] = l10
    panels_wait()
    l0 = jnp.where(r == 0, work[0], jnp.where(r == 1, work[2], dot_t(prow[0].reshape(256, 256), work[1])))
    panels[0] = l0
    panels[1] = prow[1].reshape(256, 256) - dot_t(l0, work[2])
    work[5] = dot(work[1], qcol[0].reshape(256, 256))
    work[6] = qcol[1].reshape(256, 256) - dot(work[2], work[5])

    upper0, g0 = factor_tile(rest[:128, :128])
    finish(upper0, g0, rest[128:, :], work.at[3:5])

    inv1 = work[4]
    panels[1] = jnp.where(r == 0, 0.0, jnp.where(r == 1, work[3], dot_t(panels[1], inv1)))
    u1 = jnp.where(c < 2, 0.0, dot(inv1, work[6]))
    u0 = jnp.where(c == 0, 0.0, work[5])
    mine = pl.ds(pl.multiple_of(l * 64, 64), 64)
    product = dot(panels[0, mine, :], u0) + dot(panels[1, mine, :], u1)
    half = lax.div(l, 2)
    lane = lax.broadcasted_iota(jnp.int32, (64, 256), 1)
    flag = jnp.where(lane < 128, pattern[half, 0], pattern[half, 1])
    keep = (flag > 0) | (r < 2) | (c < 2)
    schur[...] = slab[...] - jnp.where(keep, product, 0.0)

    for i in range(3):
        x_copy(i).wait_send()

    @pl.when(first)
    def _():
        for t in FIRST:
            for owner in OWNERS[0]:
                @pl.when(l != owner)
                def _():
                    d_copy(owner, t).wait_send()

    for p in range(5):
        b = PARTS[p][0]
        for owner in OWNERS[b]:
            @pl.when((l == owner) & (r == HOME[b][0]))
            def _():
                @pl.when(c == HOME[b][1])
                def _():
                    for copy in zd_copies(p, owner):
                        copy.wait_send()

                for copy in yd_copies(p, owner):
                    copy.wait_send()

            @pl.when(core == CORE[b])
            def _():
                @pl.when(l == owner)
                def _():
                    for copy in gd_copies(p, owner):
                        copy.wait_send()

                @pl.when(passes(p, owner))
                def _():
                    w_copy(p, owner).wait_send()

    @pl.when(far_row)
    def _():
        for k in range(2):
            for sender in TREE[k]:
                @pl.when(c == sender)
                def _():
                    for copy in z_copies(k)[sender]:
                        copy.wait_send()

            for copy in g_copies(prow.at[k, l], k):
                copy.wait_send()

    @pl.when(c > 0)
    def _():
        @pl.when(r < 2)
        def _():
            for copy in y_copies(0):
                copy.wait_send()

        for k in range(2):
            @pl.when(core == k)
            def _():
                for copy in g_copies(qcol.at[k, l], 2):
                    copy.wait_send()
                wq_copy(k).wait_send()


def on_device(partials, pattern):
    vmem = pl.BlockSpec(memory_space=pltpu.VMEM)
    dma = pltpu.SemaphoreType.DMA
    regular = pltpu.SemaphoreType.REGULAR
    schur, panels = pl.pallas_call(
        kernel,
        out_shape=[
            jax.ShapeDtypeStruct((64, 256), F32),
            jax.ShapeDtypeStruct((2, 256, 256), F32),
        ],
        in_specs=[pl.BlockSpec(memory_space=pltpu.SMEM), vmem],
        out_specs=[vmem] * 2,
        scratch_shapes=[
            pltpu.VMEM((4, 64, 256), F32), pltpu.VMEM((4, 1, 256, 256), F32), pltpu.VMEM((64, 256), F32),
            pltpu.VMEM((2, 4, 64, 256), F32), pltpu.VMEM((2, 4, 64, 256), F32), pltpu.VMEM((3, 256, 256), F32),
            pltpu.VMEM((7, 256, 256), F32),
            regular, regular((16,)), regular,
            dma((3,)), dma((3,)), dma((3, 3)), dma((3, 4)), dma((7,)), dma((2,)), dma((2,)), dma((7,)), dma,
            dma((5, 15)), dma((5,)), dma((5, 8)), dma((5,)), dma((5, 3)), dma((5, 4)), dma((3, 3)), dma((3, 3)),
            dma((5, 4)), dma((5, 4)), dma, dma,
        ],
        compiler_params=pltpu.CompilerParams(
            collective_id=0, has_side_effects=True, vmem_limit_bytes=32 * 1024 * 1024
        ),
        name="panels",
    )(pattern.reshape(2, 2), partials.reshape(1, 256, 256))
    return schur.reshape(1, 1, 1, 64, 1, 1, 256), panels.reshape(2, 1, 1, 256, 256)


def solution(mesh):
    return jax.shard_map(
        on_device,
        mesh=mesh,
        in_specs=(
            P("layer", None, "row", None, None, "col", None),
            P(None, "row", None, None, "col", None),
        ),
        out_specs=(
            P(None, "row", "layer", None, None, "col", None),
            P(None, None, "row", None, None),
        ),
        check_vma=False,
    )
```

```python
import jax
import jax.numpy as jnp
from jax import lax
from jax.experimental import pallas as pl
from jax.experimental.pallas import tpu as pltpu
from jax.sharding import PartitionSpec as P

MESH = pl.DeviceIdType.MESH
EXACT = lax.Precision.HIGHEST
F32 = jnp.float32


def dot(a, b):
    return lax.dot_general(a, b, (((1,), (0,)), ((), ())), precision=EXACT, preferred_element_type=F32)


def dot_t(a, b):
    return lax.dot_general(a, b, (((1,), (1,)), ((), ())), precision=EXACT, preferred_element_type=F32)


def lanes(x, k):
    return jnp.broadcast_to(x[:, k : k + 1], (8, 128))


def rows(x, k):
    return jnp.broadcast_to(x[k : k + 1, :], (8, 128))


def factor_tile(tile, side=()):
    lane=lax.broadcasted_iota(jnp.int32,(8,128),1); sub=lax.broadcasted_iota(jnp.int32,(8,128),0)
    X=[tile[8*g:8*g+8,:] for g in range(16)]; FT=[];G=[]
    for b in range(0,16,2):
        base=8*b
        Y0,Y1=X[b],X[b+1]
        c0=[lanes(Y0,base+k) for k in range(8)]
        c1=[lanes(Y1,base+k) for k in range(16)]
        Z0=jnp.where(lane<base,Y0,jnp.where(lane==base+sub,1.0,0.0))
        Z1=jnp.where(lane<base,Y1,jnp.where(lane==base+8+sub,1.0,0.0))
        U={};p=[]; dv=[None,None]; pv=[None,None]
        d=rows(c0[0],0)
        for j in range(16):
            h,q=divmod(j,8)
            dv[h]=d if q==0 else jnp.where(sub>=q,d,dv[h])
            pj=1.0/d; p.append(pj)
            pv[h]=pj if q==0 else jnp.where(sub>=q,pj,pv[h])
            if j==15: break
            if h==0:
                if j<7: e1=rows(c0[j+1],j); dn=rows(c0[j+1],j+1)
                else: e1=rows(c1[j],0); dn=rows(c1[8],0)
                d=dn-(e1*pj)*e1
                m0=jnp.where(sub>j,c0[j],0.0)*pj if j<7 else None
                m1=c1[j]*pj
                for k in range(j+1,8):
                    u=rows(c0[k],j); U[j,k]=u
                    c0[k]=c0[k]-m0*u; c1[k]=c1[k]-m1*u
                for k in range(8,16):
                    u=rows(c1[j],k-8); U[j,k]=u
                    c1[k]=c1[k]-m1*u
                y=rows(Y0,j); z=rows(Z0,j)
                if j<7: Y0=Y0-m0*y; Z0=Z0-m0*z
                Y1=Y1-m1*y; Z1=Z1-m1*z
            else:
                e1=rows(c1[j+1],q); d=rows(c1[j+1],q+1)-(e1*pj)*e1
                m1=jnp.where(sub>q,c1[j],0.0)*pj
                for k in range(j+1,16):
                    u=rows(c1[k],q); U[j,k]=u
                    c1[k]=c1[k]-m1*u
                Y1=Y1-m1*rows(Y1,q); Z1=Z1-m1*rows(Z1,q)
        for h,(Y,Z) in enumerate(((Y0,Z0),(Y1,Z1))):
            rs=lax.rsqrt(dv[h])
            FT.append(jnp.where(lane>=base+8*h+sub,Y*rs,0.0)); G.append(Z*rs)
        if b//2 < len(side):
            side[b//2]()
        if b<14:
            V0=jnp.where(lane<base+16,Z0,Y0); V1=jnp.where(lane<base+16,Z1,Y1)
            inb=(lane>=base)&(lane<base+16)
            for g in (b+2,b+3):
                cg=[lanes(X[g],base+k) for k in range(16)]
                acc=jnp.where(inb,0.0,X[g])
                for j in range(16):
                    m=cg[j]*p[j]
                    for k in range(j+1,16): cg[k]=cg[k]-m*U[j,k]
                    acc=acc-m*rows(V0 if j<8 else V1,j%8)
                X[g]=acc
            if b<12:
                K0=V0*pv[0]; K1=V1*pv[1]
                for j in range(15,0,-1):
                    h,q=divmod(j,8)
                    if h==1:
                        kr=rows(K1,q)
                        if q>0: K1=K1-jnp.where(sub<q,c1[j]*pv[1],0.0)*kr
                        col=U[0,j]
                        for i in range(1,8): col=jnp.where(sub>=i,U[i,j],col)
                        K0=K0-col*pv[0]*kr
                    else:
                        K0=K0-jnp.where(sub<q,c0[j]*pv[0],0.0)*rows(K0,q)
                parts=([jnp.zeros((base,128),F32)] if base else [])+[K0,K1,jnp.zeros((112-base,128),F32)]
                upd=dot(jnp.concatenate(X[b+4:],axis=0),jnp.concatenate(parts,axis=0))
                for g in range(b+4,16):
                    X[g]=jnp.where(inb,0.0,X[g])-upd[8*(g-b-4):8*(g-b-4)+8]
    return jnp.concatenate(FT,axis=0), jnp.concatenate(G,axis=0)


TREE = (
    {0: (1, 2, 5, 8, 15, 13), 2: (3, 4), 5: (6, 7), 8: (9, 10), 15: (14,), 13: (12, 11)},
    {1: (0, 2, 3, 6, 9, 14, 12), 3: (4, 5), 6: (7, 8), 9: (10,), 14: (15, 13), 12: (11,)},
)
COL_ORDER = (tuple(range(1, 16)), (0,) + tuple(range(2, 16)))
CHIP_ORDER = (4, 3, 5, 2, 6, 1, 7)
HOME = ((0, 0), (1, 0), (1, 1))
CORE = (0, 1, 0)
OWNERS = ((1, 2, 3), (0, 1, 2, 3), (0, 1, 2, 3))
THIRDS = {1: (0, 48), 2: (48, 88), 3: (88, 128)}
TILES = ((0, 0), (128, 0), (128, 128))
PARTS = ((0, 0), (0, 1), (0, 2), (1, 0), (2, 0))
FIRST = (0, 1, 2)
SECOND, THIRD = 3, 4


def parent_col(k, c):
    up = jnp.int32(0)
    for sender, cols in TREE[k].items():
        for col in cols:
            up = jnp.where(c == col, sender, up)
    return up


def piece(ref, p, owner):
    b, t = PARTS[p]
    if b == 0:
        lo, hi = THIRDS[owner]
        top, left = TILES[t]
        return ref.at[0, top + lo : top + hi, left : left + 128]
    if b == 2 and owner < 2:
        return ref.at[2, 64 * owner : 64 * owner + 64, 0:128]
    return ref.at[b, 64 * owner : 64 * owner + 64]


def kernel(
    pattern_hbm, part_hbm, schur, panels,
    pattern, staged, part, stage_sem, xin, din, slab, prow, qcol, lead, work,
    ready_y, ready_z, ready_w, x_send, x_recv, d_send, d_recv, z_send, zn_send, z_recv, y_send, y_recv,
    zd_send, zd_recv, yd_send, yd_recv, gd_send, gd_recv, g_send, g_recv,
    w_send, w_recv, wq_send, wq_recv,
):
    l = lax.axis_index("layer")
    r = lax.axis_index("row")
    c = lax.axis_index("col")
    core = lax.rem(r, 2)
    sibling = r + 1 - 2 * core
    peers = [lax.rem(l + d, 4) for d in (1, 2, 3)]
    far_row = r >= 2
    row_role = [(l > 0) | (c > 0), c >= 0]
    col_role = [(l > 0) | (r > 0), r > 0]

    def remote(src, dst, send, recv, device):
        return pltpu.make_async_remote_copy(
            src_ref=src, dst_ref=dst, send_sem=send, recv_sem=recv, device_id=device, device_id_type=MESH
        )

    loads = [
        pltpu.make_async_copy(part_hbm, staged, stage_sem.at[0]),
        pltpu.make_async_copy(pattern_hbm, pattern, stage_sem.at[1]),
    ]
    for load in loads:
        load.start()
    barrier = pltpu.get_barrier_semaphore()

    def greet(device):
        pl.semaphore_signal(barrier, inc=1, device_id=device, device_id_type=MESH)

    for peer in peers:
        greet((peer, r, c))

    @pl.when(core == 1)
    def _():
        greet((l, sibling, c))

    for k in range(2):
        @pl.when((c == k) & col_role[k] & jnp.logical_not(far_row))
        def _():
            for col in COL_ORDER[k]:
                greet((l, r, col))

        for sender, cols in TREE[k].items():
            @pl.when((c == sender) & far_row)
            def _():
                for col in cols:
                    greet((l, r, col))

        @pl.when((r == k) & row_role[k])
        def _():
            for y in CHIP_ORDER:
                greet((l, 2 * y + k, c))
                if k == 1:
                    greet((l, 2 * y, c))

    served_y = [far_row & row_role[0] & (core == 0), far_row & row_role[1]]
    served_z = [col_role[k] & (c != k) for k in range(2)]
    count = 3
    for flag in served_y + served_z + [core == 0]:
        count = count + jnp.where(flag, 1, 0)
    for load in loads:
        load.wait()
    for h in range(2):
        part[0, :, 128 * h : 128 * h + 128] = staged[pl.ds(h, 256, stride=2), :]
    pl.semaphore_wait(barrier, count)

    def ready(sem, device):
        pl.semaphore_signal(sem, inc=1, device_id=device, device_id_type=MESH)

    for k in range(2):
        @pl.when(served_y[k])
        def _():
            ready(ready_y, (l, k, c))

        @pl.when(served_z[k])
        def _():
            ready(ready_z.at[c], (l, r, jnp.where(far_row, parent_col(k, c), k)))

    @pl.when(core == 0)
    def _():
        ready(ready_w, (l, sibling, c))

    def d_copy(owner, t):
        return remote(piece(part, t, owner), piece(din.at[l], t, owner), d_send.at[owner - 1, t], d_recv.at[t, l],
                      (owner, r, c))

    def x_copy(i):
        rows_to = pl.ds(pl.multiple_of(peers[i] * 64, 64), 64)
        return remote(part.at[0, rows_to], xin.at[l], x_send.at[i], x_recv.at[i], (peers[i], r, c))

    first = (r == 0) & (c == 0)

    @pl.when(first)
    def _():
        for t in FIRST:
            for owner in OWNERS[0]:
                @pl.when(l != owner)
                def _():
                    d_copy(owner, t).start()

    for i in range(3):
        x_copy(i).start()

    own_rows = pl.ds(pl.multiple_of(l * 64, 64), 64)
    xin[l] = part[0, own_rows]

    def yd_rows(p):
        rows_to = [2 * y + CORE[PARTS[p][0]] for y in CHIP_ORDER]
        return rows_to + [0] if p == THIRD else rows_to

    def yd_copies(p, owner):
        ref = piece(lead, p, owner)
        return [
            remote(ref, ref, yd_send.at[p, i], yd_recv.at[p], (l, row, c)) for i, row in enumerate(yd_rows(p))
        ]

    def zd_copies(p, owner):
        ref = piece(lead, p, owner)
        return [
            remote(ref, ref, zd_send.at[p, i], zd_recv.at[p], (l, r, col))
            for i, col in enumerate(COL_ORDER[HOME[PARTS[p][0]][1]])
        ]

    def gd_copies(p, owner):
        ref = piece(lead, p, owner)
        return [remote(ref, ref, gd_send.at[p, i], gd_recv.at[p, owner], (peers[i], r, c)) for i in range(3)]

    def w_copy(p, owner):
        ref = piece(lead, p, owner)
        return remote(ref, ref, w_send.at[p, owner], w_recv.at[p, owner], (l, sibling, c))

    def row_sends(p, owner):
        for row, copy in zip(yd_rows(p), yd_copies(p, owner)):
            if row == 0:
                pl.semaphore_wait(ready_w, 1)
            copy.start()

    def col_sends(p, owner, wait):
        for col, copy in zip(COL_ORDER[HOME[PARTS[p][0]][1]], zd_copies(p, owner)):
            if wait:
                pl.semaphore_wait(ready_z.at[col], 1)
            copy.start()

    for k in range(2):
        @pl.when((r == k) & row_role[k])
        def _():
            pl.semaphore_wait(ready_y, (7, 14)[k])

    def add_first():
        for owner in OWNERS[0]:
            lo, hi = THIRDS[owner]

            @pl.when(first & (l == owner))
            def _():
                for t in FIRST:
                    top, left = TILES[t]
                    total = None
                    for q in range(4):
                        if q != owner:
                            remote(piece(part, t, owner), piece(din.at[q], t, owner), d_send.at[0, t],
                                   d_recv.at[t, q], (q, r, c)).wait_recv()
                        source = part if q == owner else din.at[q]
                        term = source[0, top + lo : top + hi, left : left + 128]
                        total = term if total is None else total + term
                    lead[0, top + lo : top + hi, left : left + 128] = total
                    row_sends(t, owner)
                    col_sends(t, owner, t == 0)

    def add_slab():
        for i in range(3):
            x_copy(i).wait_recv()
        slab[...] = (xin[0] + xin[1]) + (xin[2] + xin[3])

    @pl.when(first & (l > 0))
    def _():
        add_first()

    add_slab()

    def g_copies(ref, j):
        return [remote(ref, ref, g_send.at[j, i], g_recv.at[j, i], (peers[i], r, c)) for i in range(3)]

    def z_copies(k):
        return {
            sender: [
                remote(slab if sender == k else prow.at[k, l], prow.at[k, l],
                       z_send.at[i] if sender == k else zn_send.at[i], z_recv.at[k], (l, r, col))
                for i, col in enumerate(cols)
            ]
            for sender, cols in TREE[k].items()
        }

    def y_copies(k):
        return [
            remote(slab, qcol.at[k, l], y_send.at[i], y_recv, (l, 2 * y + k, c)) for i, y in enumerate(CHIP_ORDER)
        ]

    for p in (SECOND, THIRD):
        b = PARTS[p][0]

        @pl.when((r == 1) & (c == HOME[b][1]))
        def _():
            lead[b, own_rows] = slab[...]
            for owner in OWNERS[b]:
                @pl.when(l == owner)
                def _():
                    row_sends(p, owner)
                    col_sends(p, owner, True)

    for k in range(2):
        @pl.when((c > 0) & (r == k))
        def _():
            qcol[k, l] = slab[...]
            for copy in y_copies(k):
                copy.start()

        @pl.when(far_row & (c == k))
        def _():
            prow[k, l] = slab[...]
            for copy in g_copies(prow.at[k, l], k):
                copy.start()

    for k in (1, 0):
        for sender, cols in TREE[k].items():
            @pl.when(far_row & (c == sender))
            def _():
                copies = z_copies(k)[sender]
                if sender != k:
                    copies[0].wait_recv()
                for col, copy in zip(cols, copies):
                    pl.semaphore_wait(ready_z.at[col], 1)
                    copy.start()

    for p in (SECOND, THIRD) + FIRST:
        b = PARTS[p][0]

        @pl.when((r == HOME[b][0]) & (c != HOME[b][1]))
        def _():
            for owner in OWNERS[b]:
                @pl.when(l == owner)
                def _():
                    zd_copies(p, owner)[0].wait_recv()
                    row_sends(p, owner)

    def gather_panels():
        @pl.when(far_row)
        def _():
            for k in range(2):
                leaf = c != k
                for sender in TREE[k]:
                    leaf = leaf & (c != sender)

                @pl.when(leaf)
                def _():
                    z_copies(k)[k][0].wait_recv()

                @pl.when(c != k)
                def _():
                    for copy in g_copies(prow.at[k, l], k):
                        copy.start()

        for k in range(2):
            @pl.when((c > 0) & (core == k))
            def _():
                @pl.when(far_row)
                def _():
                    y_copies(k)[0].wait_recv()

                for copy in g_copies(qcol.at[k, l], 2):
                    copy.start()

    def gather_lead(p):
        b = PARTS[p][0]

        @pl.when(core == CORE[b])
        def _():
            for owner in OWNERS[b]:
                @pl.when(l == owner)
                def _():
                    @pl.when(far_row if b < 2 else r >= 0)
                    def _():
                        yd_copies(p, owner)[0].wait_recv()

                    for copy in gd_copies(p, owner):
                        copy.start()

    def passes(p, owner):
        return (far_row | (l != owner)) if p == THIRD else (l >= 0)

    def lead_pass(p, owner):
        b = PARTS[p][0]

        @pl.when(core == CORE[b])
        def _():
            @pl.when(l != owner)
            def _():
                gd_copies(p, owner)[0].wait_recv()

            @pl.when(passes(p, owner))
            def _():
                w_copy(p, owner).start()

    def lead_wait(p, owner):
        @pl.when((core != CORE[PARTS[p][0]]) & passes(p, owner))
        def _():
            w_copy(p, owner).wait_recv()

    def wq_copy(k):
        return remote(qcol.at[k], qcol.at[k], wq_send, wq_recv, (l, sibling, c))

    def panels_pass():
        for k in range(2):
            @pl.when((c > 0) & (core == k))
            def _():
                for copy in g_copies(qcol.at[k, l], 2):
                    copy.wait_recv()
                wq_copy(k).start()

    def panels_wait():
        @pl.when(far_row)
        def _():
            for k in range(2):
                for copy in g_copies(prow.at[k, l], k):
                    copy.wait_recv()

        for k in range(2):
            @pl.when((c > 0) & (core != k))
            def _():
                wq_copy(k).wait_recv()

    @pl.when(jnp.logical_not(far_row))
    def _():
        prow[...] = jnp.zeros_like(prow)

    @pl.when(c == 0)
    def _():
        qcol[...] = jnp.zeros_like(qcol)

    @pl.when((core == 1) & far_row)
    def _():
        pl.semaphore_wait(ready_w, 1)

    gather_panels()
    for p in (SECOND, 0, THIRD, 1, 2):
        gather_lead(p)

    def stack(a, b):
        return jnp.concatenate([a, b], axis=0)

    zero = jnp.zeros((128, 128), F32)
    for owner in OWNERS[0]:
        lead_pass(0, owner)
    for owner in OWNERS[0]:
        lead_wait(0, owner)
    up0, g0 = factor_tile(lead[0, 0:128, 0:128])
    for p in (1, 2):
        for owner in OWNERS[0]:
            lead_pass(p, owner)
    for p in (SECOND, THIRD):
        for owner in OWNERS[1]:
            lead_pass(p, owner)
    panels_pass()
    for p in (1, 2):
        for owner in OWNERS[0]:
            lead_wait(p, owner)
    for p in (SECOND, THIRD):
        for owner in OWNERS[1]:
            lead_wait(p, owner)
    low = dot_t(lead[0, 128:256, 0:128], g0)

    def a1():
        work[0, :, 0:128] = dot_t(lead[1, :, 0:128], g0)

    def a2():
        work[5, :, 0:128] = lead[1, :, 128:256] - dot_t(work[0, :, 0:128], low)

    def a3():
        top = work[0, 0:128, 0:128]
        work[1, 0:128, 0:128] = lead[2, 0:128, 0:128] - dot_t(top, top)

    def a4():
        work[1, 128:256] = lead[2, 128:256] - dot_t(work[0, 128:256, 0:128], work[0, :, 0:128])

    up1, g1 = factor_tile(lead[0, 128:256, 128:256] - dot_t(low, low), (a1, a2, a3, a4))
    l10b = dot_t(work[5, :, 0:128], g1)
    work[0, :, 128:256] = l10b
    d22 = work[1, 0:128, 0:128] - dot_t(l10b[0:128], l10b[0:128])
    panels_wait()

    def b0():
        work[1, 128:256] = work[1, 128:256] - dot_t(work[0, 128:256, 128:256], work[0, :, 128:256])

    def b1():
        x = dot_t(prow[0].reshape(256, 256)[:, 0:128], g0)
        panels[0, :, 0:128] = jnp.where(r == 0, stack(up0.T, low), jnp.where(r == 1, work[0, :, 0:128], x))
        work[3, 0:128] = dot(g0, qcol[0].reshape(256, 256)[0:128])

    def b2():
        work[5, :, 0:128] = prow[0].reshape(256, 256)[:, 128:256] - dot_t(panels[0, :, 0:128], low)
        work[6, 0:128] = qcol[0].reshape(256, 256)[128:256] - dot(low, work[3, 0:128])

    def b3():
        x = dot_t(work[5, :, 0:128], g1)
        panels[0, :, 128:256] = jnp.where(r == 0, stack(zero, up1.T), jnp.where(r == 1, work[0, :, 128:256], x))
        work[3, 128:256] = dot(g1, work[6, 0:128])

    def b4():
        work[2] = prow[1].reshape(256, 256) - dot_t(panels[0], work[0])

    def b5():
        work[4] = qcol[1].reshape(256, 256) - dot(work[0], work[3])

    up2, g2 = factor_tile(d22, (b0, b1, b2, b3, b4, b5))
    low1 = dot_t(work[1, 128:256, 0:128], g2)
    half = lax.div(l, 2)
    lane = lax.broadcasted_iota(jnp.int32, (64, 256), 1)
    flag = jnp.where(lane < 128, pattern[half, 0], pattern[half, 1])
    keep = (flag > 0) | (r < 2) | (c < 2)

    def c1():
        x = dot_t(work[2, :, 0:128], g2)
        work[5, :, 0:128] = x
        panels[1, :, 0:128] = jnp.where(r == 0, 0.0, jnp.where(r == 1, stack(up2.T, low1), x))
        work[6, 0:128] = dot(g2, work[4, 0:128])

    def c2():
        work[5, :, 128:256] = work[2, :, 128:256] - dot_t(work[5, :, 0:128], low1)
        work[6, 128:256] = work[4, 128:256] - dot(low1, work[6, 0:128])

    def c3():
        u0 = jnp.where(c == 0, 0.0, work[3])
        u1 = jnp.where(c < 2, 0.0, work[6, 0:128])
        product = dot(panels[0, own_rows, :], u0) + dot(panels[1, own_rows, 0:128], u1)
        work[4, 0:64] = slab[...] - jnp.where(keep, product, 0.0)

    up3, g3 = factor_tile(work[1, 128:256, 128:256] - dot_t(low1, low1), (c1, c2, c3))
    x = dot_t(work[5, :, 128:256], g3)
    panels[1, :, 128:256] = jnp.where(r == 0, 0.0, jnp.where(r == 1, stack(zero, up3.T), x))
    u1 = jnp.where(c < 2, 0.0, dot(g3, work[6, 128:256]))
    result = work[4, 0:64] - jnp.where(keep, dot(panels[1, own_rows, 128:256], u1), 0.0)
    for h in range(2):
        schur[pl.ds(h, 64, stride=2), :] = result[:, 128 * h : 128 * h + 128]

    for i in range(3):
        x_copy(i).wait_send()

    @pl.when(first)
    def _():
        for t in FIRST:
            for owner in OWNERS[0]:
                @pl.when(l != owner)
                def _():
                    d_copy(owner, t).wait_send()

    for p in range(5):
        b = PARTS[p][0]
        for owner in OWNERS[b]:
            @pl.when((l == owner) & (r == HOME[b][0]))
            def _():
                @pl.when(c == HOME[b][1])
                def _():
                    for copy in zd_copies(p, owner):
                        copy.wait_send()

                for copy in yd_copies(p, owner):
                    copy.wait_send()

            @pl.when(core == CORE[b])
            def _():
                @pl.when(l == owner)
                def _():
                    for copy in gd_copies(p, owner):
                        copy.wait_send()

                @pl.when(passes(p, owner))
                def _():
                    w_copy(p, owner).wait_send()

    @pl.when(far_row)
    def _():
        for k in range(2):
            for sender in TREE[k]:
                @pl.when(c == sender)
                def _():
                    for copy in z_copies(k)[sender]:
                        copy.wait_send()

            for copy in g_copies(prow.at[k, l], k):
                copy.wait_send()

    @pl.when(c > 0)
    def _():
        @pl.when(r < 2)
        def _():
            for copy in y_copies(0):
                copy.wait_send()

        for k in range(2):
            @pl.when(core == k)
            def _():
                for copy in g_copies(qcol.at[k, l], 2):
                    copy.wait_send()
                wq_copy(k).wait_send()


def on_device(partials, pattern):
    vmem = pl.BlockSpec(memory_space=pltpu.VMEM)
    dma = pltpu.SemaphoreType.DMA
    regular = pltpu.SemaphoreType.REGULAR
    schur, panels = pl.pallas_call(
        kernel,
        out_shape=[
            jax.ShapeDtypeStruct((128, 128), F32),
            jax.ShapeDtypeStruct((2, 256, 256), F32),
        ],
        in_specs=[pl.BlockSpec(memory_space=pl.ANY)] * 2,
        out_specs=[vmem] * 2,
        scratch_shapes=[
            pltpu.SMEM((2, 2), jnp.int32), pltpu.VMEM((512, 128), F32), pltpu.VMEM((1, 256, 256), F32), dma((2,)),
            pltpu.VMEM((4, 64, 256), F32), pltpu.VMEM((4, 1, 256, 256), F32), pltpu.VMEM((64, 256), F32),
            pltpu.VMEM((2, 4, 64, 256), F32), pltpu.VMEM((2, 4, 64, 256), F32), pltpu.VMEM((3, 256, 256), F32),
            pltpu.VMEM((7, 256, 256), F32),
            regular, regular((16,)), regular,
            dma((3,)), dma((3,)), dma((3, 3)), dma((3, 4)), dma((7,)), dma((2,)), dma((2,)), dma((7,)), dma,
            dma((5, 15)), dma((5,)), dma((5, 8)), dma((5,)), dma((5, 3)), dma((5, 4)), dma((3, 3)), dma((3, 3)),
            dma((5, 4)), dma((5, 4)), dma, dma,
        ],
        compiler_params=pltpu.CompilerParams(
            collective_id=0, has_side_effects=True, vmem_limit_bytes=32 * 1024 * 1024
        ),
        name="panels",
    )(pattern.reshape(2, 2), partials.reshape(512, 128))
    return schur.reshape(1, 1, 1, 64, 1, 1, 256), panels.reshape(2, 1, 1, 256, 256)


def solution(mesh):
    return jax.shard_map(
        on_device,
        mesh=mesh,
        in_specs=(
            P("layer", None, "row", None, None, "col", None),
            P(None, "row", None, None, "col", None),
        ),
        out_specs=(
            P(None, "row", "layer", None, None, "col", None),
            P(None, None, "row", None, None),
        ),
        check_vma=False,
    )
```

```python
import jax
import jax.numpy as jnp
from jax import lax
from jax.experimental import pallas as pl
from jax.experimental.pallas import tpu as pltpu
from jax.sharding import PartitionSpec as P

MESH = pl.DeviceIdType.MESH
EXACT = lax.Precision.HIGHEST
F32 = jnp.float32


def dot(a, b):
    return lax.dot_general(a, b, (((1,), (0,)), ((), ())), precision=EXACT, preferred_element_type=F32)


def dot_t(a, b):
    return lax.dot_general(a, b, (((1,), (1,)), ((), ())), precision=EXACT, preferred_element_type=F32)


def lanes(x, k):
    return jnp.broadcast_to(x[:, k : k + 1], (8, 128))


def rows(x, k):
    return jnp.broadcast_to(x[k : k + 1, :], (8, 128))


def factor_tile(tile, side=()):
    lane=lax.broadcasted_iota(jnp.int32,(8,128),1); sub=lax.broadcasted_iota(jnp.int32,(8,128),0)
    X=[tile[8*g:8*g+8,:] for g in range(16)]; FT=[];G=[]
    for b in range(0,16,2):
        base=8*b
        Y0,Y1=X[b],X[b+1]
        c0=[lanes(Y0,base+k) for k in range(8)]
        c1=[lanes(Y1,base+k) for k in range(16)]
        Z0=jnp.where(lane<base,Y0,jnp.where(lane==base+sub,1.0,0.0))
        Z1=jnp.where(lane<base,Y1,jnp.where(lane==base+8+sub,1.0,0.0))
        U={};p=[]; dv=[None,None]; pv=[None,None]
        d=rows(c0[0],0)
        for j in range(16):
            h,q=divmod(j,8)
            dv[h]=d if q==0 else jnp.where(sub>=q,d,dv[h])
            pj=1.0/d; p.append(pj)
            pv[h]=pj if q==0 else jnp.where(sub>=q,pj,pv[h])
            if j==15: break
            if h==0:
                if j<7: e1=rows(c0[j+1],j); dn=rows(c0[j+1],j+1)
                else: e1=rows(c1[j],0); dn=rows(c1[8],0)
                d=dn-(e1*pj)*e1
                m0=jnp.where(sub>j,c0[j],0.0)*pj if j<7 else None
                m1=c1[j]*pj
                for k in range(j+1,8):
                    u=rows(c0[k],j); U[j,k]=u
                    c0[k]=c0[k]-m0*u; c1[k]=c1[k]-m1*u
                for k in range(8,16):
                    u=rows(c1[j],k-8); U[j,k]=u
                    c1[k]=c1[k]-m1*u
                y=rows(Y0,j); z=rows(Z0,j)
                if j<7: Y0=Y0-m0*y; Z0=Z0-m0*z
                Y1=Y1-m1*y; Z1=Z1-m1*z
            else:
                e1=rows(c1[j+1],q); d=rows(c1[j+1],q+1)-(e1*pj)*e1
                m1=jnp.where(sub>q,c1[j],0.0)*pj
                for k in range(j+1,16):
                    u=rows(c1[k],q); U[j,k]=u
                    c1[k]=c1[k]-m1*u
                Y1=Y1-m1*rows(Y1,q); Z1=Z1-m1*rows(Z1,q)
        for h,(Y,Z) in enumerate(((Y0,Z0),(Y1,Z1))):
            rs=lax.rsqrt(dv[h])
            FT.append(jnp.where(lane>=base+8*h+sub,Y*rs,0.0)); G.append(Z*rs)
        if b//2 < len(side):
            side[b//2]()
        if b<14:
            V0=jnp.where(lane<base+16,Z0,Y0); V1=jnp.where(lane<base+16,Z1,Y1)
            inb=(lane>=base)&(lane<base+16)
            for g in (b+2,b+3):
                cg=[lanes(X[g],base+k) for k in range(16)]
                acc=jnp.where(inb,0.0,X[g])
                for j in range(16):
                    m=cg[j]*p[j]
                    for k in range(j+1,16): cg[k]=cg[k]-m*U[j,k]
                    acc=acc-m*rows(V0 if j<8 else V1,j%8)
                X[g]=acc
            if b<12:
                K0=V0*pv[0]; K1=V1*pv[1]
                for j in range(15,0,-1):
                    h,q=divmod(j,8)
                    if h==1:
                        kr=rows(K1,q)
                        if q>0: K1=K1-jnp.where(sub<q,c1[j]*pv[1],0.0)*kr
                        col=U[0,j]
                        for i in range(1,8): col=jnp.where(sub>=i,U[i,j],col)
                        K0=K0-col*pv[0]*kr
                    else:
                        K0=K0-jnp.where(sub<q,c0[j]*pv[0],0.0)*rows(K0,q)
                parts=([jnp.zeros((base,128),F32)] if base else [])+[K0,K1,jnp.zeros((112-base,128),F32)]
                upd=dot(jnp.concatenate(X[b+4:],axis=0),jnp.concatenate(parts,axis=0))
                for g in range(b+4,16):
                    X[g]=jnp.where(inb,0.0,X[g])-upd[8*(g-b-4):8*(g-b-4)+8]
    return jnp.concatenate(FT,axis=0), jnp.concatenate(G,axis=0)


TREE = (
    {0: (1, 2, 5, 8, 11, 12, 13, 14, 15), 2: (3, 4), 5: (6, 7), 8: (9, 10)},
    {1: (0, 2, 3, 6, 9, 14, 12), 3: (4, 5), 6: (7, 8), 9: (10,), 14: (15, 13), 12: (11,)},
)
COL_ORDER = (tuple(range(1, 16)), (0,) + tuple(range(2, 16)))
CHIP_ORDER = (4, 3, 5, 2, 6, 1, 7)
HOME = ((0, 0), (1, 0), (1, 1))
CORE = (0, 1, 0)
OWNERS = ((1, 2, 3), (0, 1, 2, 3), (0, 1, 2, 3))
THIRDS = {1: (0, 48), 2: (48, 88), 3: (88, 128)}
TILES = ((0, 0), (128, 0), (128, 128))
PARTS = ((0, 0), (0, 1), (0, 2), (1, 0), (2, 0))
FIRST = (0, 1, 2)
SECOND, THIRD = 3, 4


def parent_col(k, c):
    up = jnp.int32(0)
    for sender, cols in TREE[k].items():
        for col in cols:
            up = jnp.where(c == col, sender, up)
    return up


def piece(ref, p, owner):
    b, t = PARTS[p]
    if b == 0:
        lo, hi = THIRDS[owner]
        top, left = TILES[t]
        return ref.at[0, top + lo : top + hi, left : left + 128]
    if b == 2 and owner < 2:
        return ref.at[2, 64 * owner : 64 * owner + 64, 0:128]
    return ref.at[b, 64 * owner : 64 * owner + 64]


def kernel(
    pattern_hbm, part_hbm, schur, panels,
    pattern, staged, part, stage_sem, xin, din, slab, prow, qcol, lead, work,
    ready_y, ready_z, ready_w, x_send, x_recv, d_send, d_recv, z_send, zn_send, z_recv, y_send, y_recv,
    zd_send, zd_recv, yd_send, yd_recv, gd_send, gd_recv, g_send, g_recv,
    w_send, w_recv, wq_send, wq_recv,
):
    l = lax.axis_index("layer")
    r = lax.axis_index("row")
    c = lax.axis_index("col")
    core = lax.rem(r, 2)
    sibling = r + 1 - 2 * core
    peers = [lax.rem(l + d, 4) for d in (1, 2, 3)]
    far_row = r >= 2
    row_role = [(l > 0) | (c > 0), c >= 0]
    col_role = [(l > 0) | (r > 0), r > 0]

    def remote(src, dst, send, recv, device):
        return pltpu.make_async_remote_copy(
            src_ref=src, dst_ref=dst, send_sem=send, recv_sem=recv, device_id=device, device_id_type=MESH
        )

    loads = [
        pltpu.make_async_copy(part_hbm, staged, stage_sem.at[0]),
        pltpu.make_async_copy(pattern_hbm, pattern, stage_sem.at[1]),
    ]
    for load in loads:
        load.start()
    barrier = pltpu.get_barrier_semaphore()

    def greet(device):
        pl.semaphore_signal(barrier, inc=1, device_id=device, device_id_type=MESH)

    for peer in peers:
        greet((peer, r, c))

    @pl.when(core == 1)
    def _():
        greet((l, sibling, c))

    for k in range(2):
        @pl.when((c == k) & col_role[k] & jnp.logical_not(far_row))
        def _():
            for col in COL_ORDER[k]:
                greet((l, r, col))

        for sender, cols in TREE[k].items():
            @pl.when((c == sender) & far_row)
            def _():
                for col in cols:
                    greet((l, r, col))

        @pl.when((r == k) & row_role[k])
        def _():
            for y in CHIP_ORDER:
                greet((l, 2 * y + k, c))
                if k == 1:
                    greet((l, 2 * y, c))

    served_y = [far_row & row_role[0] & (core == 0), far_row & row_role[1]]
    served_z = [col_role[k] & (c != k) for k in range(2)]
    count = 3
    for flag in served_y + served_z + [core == 0]:
        count = count + jnp.where(flag, 1, 0)
    for load in loads:
        load.wait()
    for h in range(2):
        part[0, :, 128 * h : 128 * h + 128] = staged[pl.ds(h, 256, stride=2), :]
    pl.semaphore_wait(barrier, count)

    def ready(sem, device):
        pl.semaphore_signal(sem, inc=1, device_id=device, device_id_type=MESH)

    for k in range(2):
        @pl.when(served_y[k])
        def _():
            ready(ready_y, (l, k, c))

        @pl.when(served_z[k])
        def _():
            ready(ready_z.at[c], (l, r, jnp.where(far_row, parent_col(k, c), k)))

    @pl.when(core == 0)
    def _():
        ready(ready_w, (l, sibling, c))

    def d_copy(owner, t):
        return remote(piece(part, t, owner), piece(din.at[l], t, owner), d_send.at[owner - 1, t], d_recv.at[t, l],
                      (owner, r, c))

    def x_copy(i):
        rows_to = pl.ds(pl.multiple_of(peers[i] * 64, 64), 64)
        return remote(part.at[0, rows_to], xin.at[l], x_send.at[i], x_recv.at[i], (peers[i], r, c))

    first = (r == 0) & (c == 0)

    @pl.when(first)
    def _():
        for t in FIRST:
            for owner in OWNERS[0]:
                @pl.when(l != owner)
                def _():
                    d_copy(owner, t).start()

    for i in range(3):
        x_copy(i).start()

    own_rows = pl.ds(pl.multiple_of(l * 64, 64), 64)
    xin[l] = part[0, own_rows]

    def yd_rows(p):
        rows_to = [2 * y + CORE[PARTS[p][0]] for y in CHIP_ORDER]
        return rows_to + [0] if p == THIRD else rows_to

    def yd_copies(p, owner):
        ref = piece(lead, p, owner)
        return [
            remote(ref, ref, yd_send.at[p, i], yd_recv.at[p], (l, row, c)) for i, row in enumerate(yd_rows(p))
        ]

    def zd_copies(p, owner):
        ref = piece(lead, p, owner)
        return [
            remote(ref, ref, zd_send.at[p, i], zd_recv.at[p], (l, r, col))
            for i, col in enumerate(COL_ORDER[HOME[PARTS[p][0]][1]])
        ]

    def gd_copies(p, owner):
        ref = piece(lead, p, owner)
        return [remote(ref, ref, gd_send.at[p, i], gd_recv.at[p, owner], (peers[i], r, c)) for i in range(3)]

    def w_copy(p, owner):
        ref = piece(lead, p, owner)
        return remote(ref, ref, w_send.at[p, owner], w_recv.at[p, owner], (l, sibling, c))

    def row_sends(p, owner):
        for row, copy in zip(yd_rows(p), yd_copies(p, owner)):
            if row == 0:
                pl.semaphore_wait(ready_w, 1)
            copy.start()

    def col_sends(p, owner, wait):
        for col, copy in zip(COL_ORDER[HOME[PARTS[p][0]][1]], zd_copies(p, owner)):
            if wait:
                pl.semaphore_wait(ready_z.at[col], 1)
            copy.start()

    for k in range(2):
        @pl.when((r == k) & row_role[k])
        def _():
            pl.semaphore_wait(ready_y, (7, 14)[k])

    def add_first():
        for owner in OWNERS[0]:
            lo, hi = THIRDS[owner]

            @pl.when(first & (l == owner))
            def _():
                for t in FIRST:
                    top, left = TILES[t]
                    total = None
                    for q in range(4):
                        if q != owner:
                            remote(piece(part, t, owner), piece(din.at[q], t, owner), d_send.at[0, t],
                                   d_recv.at[t, q], (q, r, c)).wait_recv()
                        source = part if q == owner else din.at[q]
                        term = source[0, top + lo : top + hi, left : left + 128]
                        total = term if total is None else total + term
                    lead[0, top + lo : top + hi, left : left + 128] = total
                    row_sends(t, owner)
                    col_sends(t, owner, t == 0)

    def add_slab():
        for i in range(3):
            x_copy(i).wait_recv()
        slab[...] = (xin[0] + xin[1]) + (xin[2] + xin[3])

    @pl.when(first & (l > 0))
    def _():
        add_first()

    add_slab()

    def g_copies(ref, j):
        return [remote(ref, ref, g_send.at[j, i], g_recv.at[j, i], (peers[i], r, c)) for i in range(3)]

    def z_copies(k):
        return {
            sender: [
                remote(slab if sender == k else prow.at[k, l], prow.at[k, l],
                       z_send.at[i] if sender == k else zn_send.at[i], z_recv.at[k], (l, r, col))
                for i, col in enumerate(cols)
            ]
            for sender, cols in TREE[k].items()
        }

    def y_copies(k):
        return [
            remote(slab, qcol.at[k, l], y_send.at[i], y_recv, (l, 2 * y + k, c)) for i, y in enumerate(CHIP_ORDER)
        ]

    for p in (SECOND, THIRD):
        b = PARTS[p][0]

        @pl.when((r == 1) & (c == HOME[b][1]))
        def _():
            lead[b, own_rows] = slab[...]
            for owner in OWNERS[b]:
                @pl.when(l == owner)
                def _():
                    row_sends(p, owner)
                    col_sends(p, owner, True)

    for k in range(2):
        @pl.when((c > 0) & (r == k))
        def _():
            qcol[k, l] = slab[...]
            for copy in y_copies(k):
                copy.start()

        @pl.when(far_row & (c == k))
        def _():
            prow[k, l] = slab[...]
            for copy in g_copies(prow.at[k, l], k):
                copy.start()

    for k in (1, 0):
        for sender, cols in TREE[k].items():
            @pl.when(far_row & (c == sender))
            def _():
                copies = z_copies(k)[sender]
                if sender != k:
                    copies[0].wait_recv()
                for col, copy in zip(cols, copies):
                    pl.semaphore_wait(ready_z.at[col], 1)
                    copy.start()

    for p in (SECOND, THIRD) + FIRST:
        b = PARTS[p][0]

        @pl.when((r == HOME[b][0]) & (c != HOME[b][1]))
        def _():
            for owner in OWNERS[b]:
                @pl.when(l == owner)
                def _():
                    zd_copies(p, owner)[0].wait_recv()
                    row_sends(p, owner)

    def gather_panels():
        @pl.when(far_row)
        def _():
            for k in range(2):
                leaf = c != k
                for sender in TREE[k]:
                    leaf = leaf & (c != sender)

                @pl.when(leaf)
                def _():
                    z_copies(k)[k][0].wait_recv()

                @pl.when(c != k)
                def _():
                    for copy in g_copies(prow.at[k, l], k):
                        copy.start()

        for k in range(2):
            @pl.when((c > 0) & (core == k))
            def _():
                @pl.when(far_row)
                def _():
                    y_copies(k)[0].wait_recv()

                for copy in g_copies(qcol.at[k, l], 2):
                    copy.start()

    def gather_lead(p):
        b = PARTS[p][0]

        @pl.when(core == CORE[b])
        def _():
            for owner in OWNERS[b]:
                @pl.when(l == owner)
                def _():
                    @pl.when(far_row if b < 2 else r >= 0)
                    def _():
                        yd_copies(p, owner)[0].wait_recv()

                    for copy in gd_copies(p, owner):
                        copy.start()

    def passes(p, owner):
        return (far_row | (l != owner)) if p == THIRD else (l >= 0)

    def lead_pass(p, owner):
        b = PARTS[p][0]

        @pl.when(core == CORE[b])
        def _():
            @pl.when(l != owner)
            def _():
                gd_copies(p, owner)[0].wait_recv()

            @pl.when(passes(p, owner))
            def _():
                w_copy(p, owner).start()

    def lead_wait(p, owner):
        @pl.when((core != CORE[PARTS[p][0]]) & passes(p, owner))
        def _():
            w_copy(p, owner).wait_recv()

    def wq_copy(k):
        return remote(qcol.at[k], qcol.at[k], wq_send, wq_recv, (l, sibling, c))

    def panels_pass():
        for k in range(2):
            @pl.when((c > 0) & (core == k))
            def _():
                for copy in g_copies(qcol.at[k, l], 2):
                    copy.wait_recv()
                wq_copy(k).start()

    def panels_wait():
        @pl.when(far_row)
        def _():
            for k in range(2):
                for copy in g_copies(prow.at[k, l], k):
                    copy.wait_recv()

        for k in range(2):
            @pl.when((c > 0) & (core != k))
            def _():
                wq_copy(k).wait_recv()

    @pl.when(jnp.logical_not(far_row))
    def _():
        prow[...] = jnp.zeros_like(prow)

    @pl.when(c == 0)
    def _():
        qcol[...] = jnp.zeros_like(qcol)

    @pl.when((core == 1) & far_row)
    def _():
        pl.semaphore_wait(ready_w, 1)

    gather_panels()
    for p in (SECOND, 0, THIRD, 1, 2):
        gather_lead(p)

    def stack(a, b):
        return jnp.concatenate([a, b], axis=0)

    zero = jnp.zeros((128, 128), F32)
    for owner in OWNERS[0]:
        lead_pass(0, owner)
    for owner in OWNERS[0]:
        lead_wait(0, owner)
    up0, g0 = factor_tile(lead[0, 0:128, 0:128])
    for p in (1, 2):
        for owner in OWNERS[0]:
            lead_pass(p, owner)
    for p in (SECOND, THIRD):
        for owner in OWNERS[1]:
            lead_pass(p, owner)
    panels_pass()
    for p in (1, 2):
        for owner in OWNERS[0]:
            lead_wait(p, owner)
    for p in (SECOND, THIRD):
        for owner in OWNERS[1]:
            lead_wait(p, owner)
    low = dot_t(lead[0, 128:256, 0:128], g0)

    def a1():
        work[0, :, 0:128] = dot_t(lead[1, :, 0:128], g0)

    def a2():
        work[5, :, 0:128] = lead[1, :, 128:256] - dot_t(work[0, :, 0:128], low)

    def a3():
        top = work[0, 0:128, 0:128]
        work[1, 0:128, 0:128] = lead[2, 0:128, 0:128] - dot_t(top, top)

    def a4():
        work[1, 128:256] = lead[2, 128:256] - dot_t(work[0, 128:256, 0:128], work[0, :, 0:128])

    up1, g1 = factor_tile(lead[0, 128:256, 128:256] - dot_t(low, low), (a1, a2, a3, a4))
    l10b = dot_t(work[5, :, 0:128], g1)
    work[0, :, 128:256] = l10b
    d22 = work[1, 0:128, 0:128] - dot_t(l10b[0:128], l10b[0:128])
    panels_wait()

    def b0():
        work[1, 128:256] = work[1, 128:256] - dot_t(work[0, 128:256, 128:256], work[0, :, 128:256])

    def b1():
        x = dot_t(prow[0].reshape(256, 256)[:, 0:128], g0)
        panels[0, :, 0:128] = jnp.where(r == 0, stack(up0.T, low), jnp.where(r == 1, work[0, :, 0:128], x))
        work[3, 0:128] = dot(g0, qcol[0].reshape(256, 256)[0:128])

    def b2():
        work[5, :, 0:128] = prow[0].reshape(256, 256)[:, 128:256] - dot_t(panels[0, :, 0:128], low)
        work[6, 0:128] = qcol[0].reshape(256, 256)[128:256] - dot(low, work[3, 0:128])

    def b3():
        x = dot_t(work[5, :, 0:128], g1)
        panels[0, :, 128:256] = jnp.where(r == 0, stack(zero, up1.T), jnp.where(r == 1, work[0, :, 128:256], x))
        work[3, 128:256] = dot(g1, work[6, 0:128])

    def b4():
        work[2] = prow[1].reshape(256, 256) - dot_t(panels[0], work[0])

    def b5():
        work[4] = qcol[1].reshape(256, 256) - dot(work[0], work[3])

    up2, g2 = factor_tile(d22, (b0, b1, b2, b3, b4, b5))
    low1 = dot_t(work[1, 128:256, 0:128], g2)
    half = lax.div(l, 2)
    lane = lax.broadcasted_iota(jnp.int32, (64, 256), 1)
    flag = jnp.where(lane < 128, pattern[half, 0], pattern[half, 1])
    keep = (flag > 0) | (r < 2) | (c < 2)

    def c1():
        x = dot_t(work[2, :, 0:128], g2)
        work[5, :, 0:128] = x
        panels[1, :, 0:128] = jnp.where(r == 0, 0.0, jnp.where(r == 1, stack(up2.T, low1), x))
        work[6, 0:128] = dot(g2, work[4, 0:128])

    def c2():
        work[5, :, 128:256] = work[2, :, 128:256] - dot_t(work[5, :, 0:128], low1)
        work[6, 128:256] = work[4, 128:256] - dot(low1, work[6, 0:128])

    def c3():
        u0 = jnp.where(c == 0, 0.0, work[3])
        u1 = jnp.where(c < 2, 0.0, work[6, 0:128])
        product = dot(panels[0, own_rows, :], u0) + dot(panels[1, own_rows, 0:128], u1)
        work[4, 0:64] = slab[...] - jnp.where(keep, product, 0.0)

    up3, g3 = factor_tile(work[1, 128:256, 128:256] - dot_t(low1, low1), (c1, c2, c3))
    x = dot_t(work[5, :, 128:256], g3)
    panels[1, :, 128:256] = jnp.where(r == 0, 0.0, jnp.where(r == 1, stack(zero, up3.T), x))
    u1 = jnp.where(c < 2, 0.0, dot(g3, work[6, 128:256]))
    result = work[4, 0:64] - jnp.where(keep, dot(panels[1, own_rows, 128:256], u1), 0.0)
    for h in range(2):
        schur[pl.ds(h, 64, stride=2), :] = result[:, 128 * h : 128 * h + 128]

    for i in range(3):
        x_copy(i).wait_send()

    @pl.when(first)
    def _():
        for t in FIRST:
            for owner in OWNERS[0]:
                @pl.when(l != owner)
                def _():
                    d_copy(owner, t).wait_send()

    for p in range(5):
        b = PARTS[p][0]
        for owner in OWNERS[b]:
            @pl.when((l == owner) & (r == HOME[b][0]))
            def _():
                @pl.when(c == HOME[b][1])
                def _():
                    for copy in zd_copies(p, owner):
                        copy.wait_send()

                for copy in yd_copies(p, owner):
                    copy.wait_send()

            @pl.when(core == CORE[b])
            def _():
                @pl.when(l == owner)
                def _():
                    for copy in gd_copies(p, owner):
                        copy.wait_send()

                @pl.when(passes(p, owner))
                def _():
                    w_copy(p, owner).wait_send()

    @pl.when(far_row)
    def _():
        for k in range(2):
            for sender in TREE[k]:
                @pl.when(c == sender)
                def _():
                    for copy in z_copies(k)[sender]:
                        copy.wait_send()

            for copy in g_copies(prow.at[k, l], k):
                copy.wait_send()

    @pl.when(c > 0)
    def _():
        @pl.when(r < 2)
        def _():
            for copy in y_copies(0):
                copy.wait_send()

        for k in range(2):
            @pl.when(core == k)
            def _():
                for copy in g_copies(qcol.at[k, l], 2):
                    copy.wait_send()
                wq_copy(k).wait_send()


def on_device(partials, pattern):
    vmem = pl.BlockSpec(memory_space=pltpu.VMEM)
    dma = pltpu.SemaphoreType.DMA
    regular = pltpu.SemaphoreType.REGULAR
    schur, panels = pl.pallas_call(
        kernel,
        out_shape=[
            jax.ShapeDtypeStruct((128, 128), F32),
            jax.ShapeDtypeStruct((2, 256, 256), F32),
        ],
        in_specs=[pl.BlockSpec(memory_space=pltpu.HBM)] * 2,
        out_specs=[vmem] * 2,
        scratch_shapes=[
            pltpu.SMEM((2, 2), jnp.int32), pltpu.VMEM((512, 128), F32), pltpu.VMEM((1, 256, 256), F32), dma((2,)),
            pltpu.VMEM((4, 64, 256), F32), pltpu.VMEM((4, 1, 256, 256), F32), pltpu.VMEM((64, 256), F32),
            pltpu.VMEM((2, 4, 64, 256), F32), pltpu.VMEM((2, 4, 64, 256), F32), pltpu.VMEM((3, 256, 256), F32),
            pltpu.VMEM((7, 256, 256), F32),
            regular, regular((16,)), regular,
            dma((3,)), dma((3,)), dma((3, 3)), dma((3, 4)), dma((9,)), dma((2,)), dma((2,)), dma((7,)), dma,
            dma((5, 15)), dma((5,)), dma((5, 8)), dma((5,)), dma((5, 3)), dma((5, 4)), dma((3, 3)), dma((3, 3)),
            dma((5, 4)), dma((5, 4)), dma, dma,
        ],
        compiler_params=pltpu.CompilerParams(
            collective_id=0, has_side_effects=True, vmem_limit_bytes=32 * 1024 * 1024
        ),
        name="panels",
    )(pattern.reshape(2, 2), partials.reshape(512, 128))
    return schur.reshape(1, 1, 1, 64, 1, 1, 256), panels.reshape(2, 1, 1, 256, 256)


def solution(mesh):
    return jax.shard_map(
        on_device,
        mesh=mesh,
        in_specs=(
            P("layer", None, "row", None, None, "col", None),
            P(None, "row", None, None, "col", None),
        ),
        out_specs=(
            P(None, "row", "layer", None, None, "col", None),
            P(None, None, "row", None, None),
        ),
        check_vma=False,
    )
```
